32 devices in a mesh: rows: 8 (over z, x), mem: 4 (over y, core).
Axes of the slice: x: 2, y: 2, z: 4, core: 2. Of those that a mesh axis runs over, the one named last changes fastest.
Arguments:
- factor_panel: float32 [8, 8, 128, 2048], P(None, 'rows'), may hold values from -0.125 to 0.125
- right_side: float32 [8, 8, 128, 128], P(None, 'rows', None, 'mem'), may hold values from -6 to 6
- inverses: float32 [4, 512, 512], replicated, may hold values from -0.125 to 1.5, as said below
Outputs:
- solved: float32 [2048, 128], P(None, 'mem')
- remainder: float32 [8, 8, 128, 128], P(None, 'rows', None, 'mem')
- spread: float32 [8, 8, 128], P(None, 'rows')
The draws below stay inside these ranges and needn't reach their ends.
Inputs may be any that keep to these rules, and one draw needn't show every extreme that they name: `inverses`: each block is lower triangular with its diagonal between 0.5 and 1.5 and its entries below the diagonal between -0.125 and 0.125.
All inputs are finite; a program needn't handle non-finite values.
Results may differ from the reference program's by a relative error of at most 0.0001.
Values sent between devices are 32-bit elements; how exact they have to be, the bound alone decides.
A program may use at most 64 MiB of HBM per device.

```python
import math
import jax
import jax.numpy as jnp
from jax import lax

TILE = 128
STEP_W = 512
STEPS = 4
TILE_BLOCKS = 8
COLS = 2048
MEMBERS = 128
N_ROWS = 8


def draw_inverses(key, part):
    diag_key, below_key = jax.random.split(jax.random.fold_in(key, 7))
    diagonal = jax.random.uniform(diag_key, (STEPS, STEP_W), jnp.float32, 0.5, 1.5)
    below = jnp.clip(jax.random.normal(below_key, (STEPS, STEP_W, STEP_W), jnp.float32), -4.0, 4.0)
    below = jnp.clip(below * (0.6 / math.sqrt(STEP_W)), -0.125, 0.125)
    below = jnp.tril(below, -1)
    identity = jnp.eye(STEP_W, dtype=jnp.float32)
    return below + identity[None] * diagonal[:, :, None]


def level_of(stream_key, shape, cuts, least, largest):
    def one(axis_at, shards_of):
        draws = jax.random.uniform(jax.random.fold_in(jax.random.fold_in(stream_key, 6), axis_at), (shards_of,), jnp.float32, least / len(cuts), largest / len(cuts))
        return jnp.repeat(jnp.exp(draws), shape[axis_at] // shards_of).reshape((-1,) + (1,) * (len(shape) - axis_at - 1))

    factor_of = one(*cuts[0])
    for cut in cuts[1:]:
        factor_of = factor_of * one(*cut)
    return factor_of


def noise(key, extent, scale, bound, cuts=(), kind=jnp.bfloat16):
    result = jax.random.normal(key, extent, jnp.float32) * scale
    if len(cuts) > 0:
        result = level_of(key, extent, cuts, -0.22, 0.18) * result
    return jnp.clip(result, min=-bound, max=bound).astype(kind)


def setup_inputs(seed: int = 0) -> dict:
    key_list = jax.random.split(jax.random.key(seed), 4)
    return {
        "factor_panel": noise(key_list[0], (TILE_BLOCKS, N_ROWS, TILE, COLS), COLS ** -0.5, 0.125, ((1, 8),), jnp.float32),
        "right_side": noise(key_list[1], (TILE_BLOCKS, N_ROWS, TILE, MEMBERS), 1.0, 6.0, ((1, 8), (3, 4)), jnp.float32),
        "inverses": draw_inverses(jax.random.fold_in(key_list[3], 71), 0),
    }


highest = lax.Precision.HIGHEST


def reference(factor_panel, right_side, inverses):
    lower_rows = factor_panel.reshape(-1, COLS)
    right_rows = right_side.reshape(-1, MEMBERS)
    row_ids = jnp.arange(COLS, dtype=jnp.int32)
    limits = (row_ids // STEP_W) * STEP_W
    column_ids = jnp.arange(COLS, dtype=jnp.int32)
    masked_head = jnp.where(column_ids[None, :] < limits[:, None], lower_rows[:COLS], jnp.float32(0.0))
    blocks = []
    for section in range(STEPS):
        start = section * STEP_W
        residual = right_rows[start:start + STEP_W]
        if section > 0:
            earlier = jnp.concatenate(blocks, axis=0)
            residual = residual - jnp.dot(masked_head[start:start + STEP_W, :start], earlier, precision=highest, preferred_element_type=jnp.float32)
        blocks.append(jnp.dot(inverses[section], residual, precision=highest, preferred_element_type=jnp.float32))
    solved = jnp.concatenate(blocks, axis=0)
    head_left = right_rows[:COLS] - jnp.dot(masked_head, solved, precision=highest, preferred_element_type=jnp.float32)
    tail_left = right_rows[COLS:] - jnp.dot(lower_rows[COLS:], solved, precision=highest, preferred_element_type=jnp.float32)
    remainder = jnp.concatenate([head_left, tail_left], axis=0)
    member_mean = jnp.sum(remainder, axis=1) / MEMBERS
    spread = jnp.sum(remainder * remainder, axis=1) / MEMBERS - member_mean * member_mean
    return solved, remainder.reshape(right_side.shape), spread.reshape(TILE_BLOCKS, N_ROWS, TILE)
```

```python
import functools

import jax
import jax.numpy as jnp
from jax import lax
from jax.experimental import pallas as pl
from jax.experimental.pallas import tpu as pltpu
from jax.sharding import PartitionSpec as P

f32 = jnp.float32
bf16 = jnp.bfloat16
MESH = pl.DeviceIdType.MESH


def split(x):
    high = x.astype(bf16)
    return high, (x - high.astype(f32)).astype(bf16)


def dot_nt(a, b):
    return lax.dot_general(a, b, (((1,), (1,)), ((), ())), preferred_element_type=f32)


def dot_nn(a, b):
    return lax.dot_general(a, b, (((1,), (0,)), ((), ())), preferred_element_type=f32)


def product(stacked, weight_high, weight_low, dot=dot_nt):
    half = stacked.shape[0] // 2
    both = dot(stacked, weight_high)
    return both[:half] + both[half:] + dot(stacked[:half], weight_low)


def stack(x):
    return jnp.concatenate(split(x), axis=0)


def kernel(
    row_devices,
    mem_devices,
    panel_hbm,
    right_hbm,
    inverse_hbm,
    solved,
    left,
    spread_ref,
    panel,
    inverse,
    pieces,
    gain_high,
    gain_low,
    sums,
    panel_sem,
    inverse_sem,
    right_sem,
    send_sem,
    recv_sem,
    sums_send_sem,
    sums_recv_sem,
):
    p = lax.axis_index("rows")
    m = lax.axis_index("mem")
    steps, tile_blocks, tile, width = panel.shape
    tiles = width // tile
    heads = min(tile_blocks, -(-(steps * tiles) // row_devices))
    members = left.shape[1]

    load_right = pltpu.make_async_copy(right_hbm, left, right_sem)
    load_right.start()
    load_panel, load_inverse = [], []
    for s in range(steps):
        load_inverse.append(
            pltpu.make_async_copy(inverse_hbm.at[s], inverse.at[s], inverse_sem.at[s])
        )
        load_inverse[s].start()
        load_panel.append(
            pltpu.make_async_copy(
                panel_hbm.at[:, :, pl.ds(s * width, width)], panel.at[s], panel_sem.at[s]
            )
        )
        load_panel[s].start()

    barrier = pltpu.get_barrier_semaphore()
    for k in range(1, row_devices):
        pl.semaphore_signal(
            barrier, inc=1, device_id=(lax.rem(p + k, row_devices), m), device_id_type=MESH
        )
    for k in range(1, mem_devices):
        pl.semaphore_signal(
            barrier, inc=1, device_id=(p, lax.rem(m + k, mem_devices)), device_id_type=MESH
        )
    load_right.wait()
    pl.semaphore_wait(barrier, row_devices + mem_devices - 2)

    def owner(s):
        place = p - (s * tiles) % row_devices
        return place, jnp.logical_and(place >= 0, place < tiles)

    def slot_of(s):
        return (s * tiles) // row_devices

    def copy_to(s, place, k):
        target = ((s + 1) * tiles + k) % row_devices
        return target, pltpu.make_async_remote_copy(
            src_ref=pieces.at[s, place],
            dst_ref=pieces.at[s, place],
            send_sem=send_sem.at[s, k],
            recv_sem=recv_sem.at[s, place],
            device_id=(target, m),
            device_id_type=MESH,
        )

    def send(s, residual):
        place, _ = owner(s)
        pieces[s, place] = residual
        for k in range(row_devices):
            target, copy = copy_to(s, place, k)

            @pl.when(target != p)
            def _():
                copy.start()

    def receive(s):
        for i in range(tiles):
            source = (s * tiles) % row_devices + i

            @pl.when(source != p)
            def _():
                pltpu.make_async_remote_copy(
                    src_ref=pieces.at[s, i],
                    dst_ref=pieces.at[s, i],
                    send_sem=send_sem.at[s, 0],
                    recv_sem=recv_sem.at[s, i],
                    device_id=(source, m),
                    device_id_type=MESH,
                ).wait_recv()

        return stack(jnp.concatenate([pieces[s, i] for i in range(tiles)], axis=1))

    def make_gain(s):
        load_inverse[s].wait()
        load_panel[s].wait()
        if s + 1 < steps:
            _, mine = owner(s + 1)

            @pl.when(mine)
            def _():
                high, low = split(inverse[s])
                gain = product(stack(panel[s, slot_of(s + 1)]), high, low, dot_nn)
                gain_high[s], gain_low[s] = split(gain)

    _, first = owner(0)

    @pl.when(first)
    def _():
        send(0, left[slot_of(0)])

    for s in range(steps):
        make_gain(s)
        residual = receive(s)
        if s + 1 < steps:
            _, mine = owner(s + 1)

            @pl.when(mine)
            def _():
                slot = slot_of(s + 1)
                new = left[slot] - product(residual, gain_high[s], gain_low[s])
                left[slot] = new
                send(s + 1, new)

        high, low = split(inverse[s])
        block = product(residual, high, low)
        solved[:, s * width : (s + 1) * width] = block
        block = stack(block)
        for j in range(heads):
            level = (j * row_devices + p) // tiles
            due = level > s + 1 if s + 1 < steps else level >= steps

            @pl.when(due)
            def _():
                high, low = split(panel[s, j])
                left[j] = left[j] - product(block, high, low)

        for j in range(heads, tile_blocks, 2):
            count = min(2, tile_blocks - j)
            high, low = split(panel[s, j : j + count].reshape(count * tile, width))
            change = product(block, high, low)
            for i in range(count):
                left[j + i] = left[j + i] - change[:, i * tile : (i + 1) * tile]

    value = left[...]
    sums[m] = jnp.stack([jnp.sum(value, axis=1), jnp.sum(value * value, axis=1)])

    def sums_copy(k):
        return pltpu.make_async_remote_copy(
            src_ref=sums.at[m],
            dst_ref=sums.at[m],
            send_sem=sums_send_sem.at[k],
            recv_sem=sums_recv_sem.at[m],
            device_id=(p, lax.rem(m + k, mem_devices)),
            device_id_type=MESH,
        )

    for k in range(1, mem_devices):
        sums_copy(k).start()
    for s in range(steps):
        place, mine = owner(s)

        @pl.when(mine)
        def _():
            for k in range(row_devices):
                target, copy = copy_to(s, place, k)

                @pl.when(target != p)
                def _():
                    copy.wait_send()

    for k in range(1, mem_devices):
        other = lax.rem(m + k, mem_devices)
        pltpu.make_async_remote_copy(
            src_ref=sums.at[other],
            dst_ref=sums.at[other],
            send_sem=sums_send_sem.at[k],
            recv_sem=sums_recv_sem.at[other],
            device_id=(p, other),
            device_id_type=MESH,
        ).wait_recv()
    total = sums[0]
    for k in range(1, mem_devices):
        total = total + sums[k]
    mean = total / (members * mem_devices)
    spread_ref[...] = mean[1] - mean[0] * mean[0]
    for k in range(1, mem_devices):
        sums_copy(k).wait_send()


def shards(row_devices, mem_devices, factor_panel, right_side, inverses):
    tile_blocks, _, tile, columns = factor_panel.shape
    members = right_side.shape[3]
    steps, width, _ = inverses.shape
    tiles = width // tile
    panel = factor_panel.reshape(tile_blocks, tile, columns)
    right = jnp.swapaxes(right_side.reshape(tile_blocks, tile, members), 1, 2)
    hbm = pl.BlockSpec(memory_space=pltpu.HBM)
    vmem = pl.BlockSpec(memory_space=pltpu.VMEM)
    dma = pltpu.SemaphoreType.DMA
    solved, remainder, spread = pl.pallas_call(
        functools.partial(kernel, row_devices, mem_devices),
        out_shape=(
            jax.ShapeDtypeStruct((members, columns), f32),
            jax.ShapeDtypeStruct((tile_blocks, members, tile), f32),
            jax.ShapeDtypeStruct((tile_blocks, tile), f32),
        ),
        in_specs=[hbm] * 3,
        out_specs=(vmem, vmem, vmem),
        scratch_shapes=[
            pltpu.VMEM((steps, tile_blocks, tile, width), f32),
            pltpu.VMEM((steps, width, width), f32),
            pltpu.VMEM((steps, tiles, members, tile), f32),
            pltpu.VMEM((steps, tile, width), bf16),
            pltpu.VMEM((steps, tile, width), bf16),
            pltpu.VMEM((mem_devices, 2, tile_blocks, tile), f32),
            dma((steps,)),
            dma((steps,)),
            dma,
            dma((steps, row_devices)),
            dma((steps, tiles)),
            dma((mem_devices,)),
            dma((mem_devices,)),
        ],
        compiler_params=pltpu.CompilerParams(
            collective_id=0, has_side_effects=True, vmem_limit_bytes=48 * 1024 * 1024
        ),
    )(panel, right, inverses)
    return (
        solved.T,
        jnp.swapaxes(remainder, 1, 2).reshape(right_side.shape),
        spread.reshape(tile_blocks, 1, tile),
    )


def solution(mesh):
    return jax.shard_map(
        functools.partial(shards, mesh.shape["rows"], mesh.shape["mem"]),
        mesh=mesh,
        in_specs=(P(None, "rows", None, None), P(None, "rows", None, "mem"), P()),
        out_specs=(P(None, "mem"), P(None, "rows", None, "mem"), P(None, "rows", None)),
        check_vma=False,
    )
```

```python
import functools

import jax
import jax.numpy as jnp
from jax import lax
from jax.experimental import pallas as pl
from jax.experimental.pallas import tpu as pltpu
from jax.sharding import PartitionSpec as P

f32 = jnp.float32
bf16 = jnp.bfloat16
MESH = pl.DeviceIdType.MESH


def split(x):
    high = x.astype(bf16)
    return high, (x - high.astype(f32)).astype(bf16)


def dot_nt(a, b):
    return lax.dot_general(a, b, (((1,), (1,)), ((), ())), preferred_element_type=f32)


def dot_nn(a, b):
    return lax.dot_general(a, b, (((1,), (0,)), ((), ())), preferred_element_type=f32)


def product(stacked, weight_high, weight_low, dot=dot_nt):
    half = stacked.shape[0] // 2
    both = dot(stacked, weight_high)
    return both[:half] + both[half:] + dot(stacked[:half], weight_low)


def stack(x):
    return jnp.concatenate(split(x), axis=0)


def kernel(
    row_devices,
    mem_devices,
    panel_hbm,
    right_hbm,
    inverse_hbm,
    solved,
    left,
    spread_ref,
    panel,
    inverse,
    pieces,
    gain_high,
    gain_low,
    sums,
    panel_sem,
    inverse_sem,
    right_sem,
    send_sem,
    recv_sem,
    sums_send_sem,
    sums_recv_sem,
):
    p = lax.axis_index("rows")
    m = lax.axis_index("mem")
    steps, tile_blocks, tile, width = panel.shape
    tiles = width // tile
    heads = min(tile_blocks, -(-(steps * tiles) // row_devices))
    members = left.shape[1]

    load_right = pltpu.make_async_copy(right_hbm, left, right_sem)
    load_right.start()
    load_panel, load_inverse = [], []
    for s in range(steps):
        load_inverse.append(
            pltpu.make_async_copy(inverse_hbm.at[s], inverse.at[s], inverse_sem.at[s])
        )
        load_inverse[s].start()
        load_panel.append(
            pltpu.make_async_copy(
                panel_hbm.at[:, :, pl.ds(s * width, width)], panel.at[s], panel_sem.at[s]
            )
        )
        load_panel[s].start()

    barrier = pltpu.get_barrier_semaphore()
    for k in range(1, row_devices):
        pl.semaphore_signal(
            barrier, inc=1, device_id=(lax.rem(p + k, row_devices), m), device_id_type=MESH
        )
    for k in range(1, mem_devices):
        pl.semaphore_signal(
            barrier, inc=1, device_id=(p, lax.rem(m + k, mem_devices)), device_id_type=MESH
        )
    load_right.wait()
    pl.semaphore_wait(barrier, row_devices + mem_devices - 2)

    def owner(s):
        place = p - (s * tiles) % row_devices
        return place, jnp.logical_and(place >= 0, place < tiles)

    def slot_of(s):
        return (s * tiles) // row_devices

    def copy_to(s, place, k):
        target = ((s + 1) * tiles + k) % row_devices
        return target, pltpu.make_async_remote_copy(
            src_ref=pieces.at[s, place],
            dst_ref=pieces.at[s, place],
            send_sem=send_sem.at[s, k],
            recv_sem=recv_sem.at[s, place],
            device_id=(target, m),
            device_id_type=MESH,
        )

    def send(s, residual):
        place, _ = owner(s)
        pieces[s, place] = residual
        for k in range(row_devices):
            target, copy = copy_to(s, place, k)

            @pl.when(target != p)
            def _():
                copy.start()

    def receive(s):
        for i in range(tiles):
            source = (s * tiles) % row_devices + i

            @pl.when(source != p)
            def _():
                pltpu.make_async_remote_copy(
                    src_ref=pieces.at[s, i],
                    dst_ref=pieces.at[s, i],
                    send_sem=send_sem.at[s, 0],
                    recv_sem=recv_sem.at[s, i],
                    device_id=(source, m),
                    device_id_type=MESH,
                ).wait_recv()

        return stack(jnp.concatenate([pieces[s, i] for i in range(tiles)], axis=1))

    def make_gain(s):
        load_inverse[s].wait()
        load_panel[s].wait()
        if s + 1 < steps:
            _, mine = owner(s + 1)

            @pl.when(mine)
            def _():
                high, low = split(inverse[s])
                gain = product(stack(panel[s, slot_of(s + 1)]), high, low, dot_nn)
                gain_high[s], gain_low[s] = split(gain)

    _, first = owner(0)

    @pl.when(first)
    def _():
        send(0, left[slot_of(0)])

    for s in range(steps):
        make_gain(s)
        residual = receive(s)
        if s + 1 < steps:
            _, mine = owner(s + 1)

            @pl.when(mine)
            def _():
                slot = slot_of(s + 1)
                new = left[slot] - product(residual, gain_high[s], gain_low[s])
                left[slot] = new
                send(s + 1, new)

        high, low = split(inverse[s])
        block = product(residual, high, low)
        solved[:, s * width : (s + 1) * width] = block
        block = stack(block)
        for j in range(heads):
            level = (j * row_devices + p) // tiles
            due = level > s + 1 if s + 1 < steps else level >= steps

            @pl.when(due)
            def _():
                high, low = split(panel[s, j])
                left[j] = left[j] - product(block, high, low)

        for j in range(heads, tile_blocks, 2):
            count = min(2, tile_blocks - j)
            high, low = split(panel[s, j : j + count].reshape(count * tile, width))
            change = product(block, high, low)
            for i in range(count):
                left[j + i] = left[j + i] - change[:, i * tile : (i + 1) * tile]

    value = left[...]
    sums[m] = jnp.stack([jnp.sum(value, axis=1), jnp.sum(value * value, axis=1)])

    def sums_copy(k):
        return pltpu.make_async_remote_copy(
            src_ref=sums.at[m],
            dst_ref=sums.at[m],
            send_sem=sums_send_sem.at[k],
            recv_sem=sums_recv_sem.at[m],
            device_id=(p, lax.rem(m + k, mem_devices)),
            device_id_type=MESH,
        )

    for k in range(1, mem_devices):
        sums_copy(k).start()
    for s in range(steps):
        place, mine = owner(s)

        @pl.when(mine)
        def _():
            for k in range(row_devices):
                target, copy = copy_to(s, place, k)

                @pl.when(target != p)
                def _():
                    copy.wait_send()

    for k in range(1, mem_devices):
        other = lax.rem(m + k, mem_devices)
        pltpu.make_async_remote_copy(
            src_ref=sums.at[other],
            dst_ref=sums.at[other],
            send_sem=sums_send_sem.at[k],
            recv_sem=sums_recv_sem.at[other],
            device_id=(p, other),
            device_id_type=MESH,
        ).wait_recv()
    total = sums[0]
    for k in range(1, mem_devices):
        total = total + sums[k]
    mean = total / (members * mem_devices)
    spread_ref[...] = mean[1] - mean[0] * mean[0]
    for k in range(1, mem_devices):
        sums_copy(k).wait_send()


def store_kernel(*refs):
    count = (len(refs) - 1) // 2
    copies = [
        pltpu.make_async_copy(refs[i], refs[count + i], refs[-1].at[i]) for i in range(count)
    ]
    for copy in copies:
        copy.start()
    for copy in copies:
        copy.wait()


def store(*arrays):
    spec = pl.BlockSpec(memory_space=pl.ANY)
    return pl.pallas_call(
        store_kernel,
        out_shape=tuple(jax.ShapeDtypeStruct(a.shape, a.dtype) for a in arrays),
        in_specs=[spec] * len(arrays),
        out_specs=(spec,) * len(arrays),
        scratch_shapes=[pltpu.SemaphoreType.DMA((len(arrays),))],
        compiler_params=pltpu.CompilerParams(vmem_limit_bytes=1024 * 1024),
    )(*arrays)


def shards(row_devices, mem_devices, factor_panel, right_side, inverses):
    tile_blocks, _, tile, columns = factor_panel.shape
    members = right_side.shape[3]
    steps, width, _ = inverses.shape
    tiles = width // tile
    panel = factor_panel.reshape(tile_blocks, tile, columns)
    right = jnp.swapaxes(right_side.reshape(tile_blocks, tile, members), 1, 2)
    hbm = pl.BlockSpec(memory_space=pltpu.HBM)
    vmem = pl.BlockSpec(memory_space=pltpu.VMEM)
    dma = pltpu.SemaphoreType.DMA
    solved, remainder, spread = pl.pallas_call(
        functools.partial(kernel, row_devices, mem_devices),
        out_shape=(
            jax.ShapeDtypeStruct((members, columns), f32),
            jax.ShapeDtypeStruct((tile_blocks, members, tile), f32),
            jax.ShapeDtypeStruct((tile_blocks, tile), f32),
        ),
        in_specs=[hbm] * 3,
        out_specs=(vmem, vmem, vmem),
        scratch_shapes=[
            pltpu.VMEM((steps, tile_blocks, tile, width), f32),
            pltpu.VMEM((steps, width, width), f32),
            pltpu.VMEM((steps, tiles, members, tile), f32),
            pltpu.VMEM((steps, tile, width), bf16),
            pltpu.VMEM((steps, tile, width), bf16),
            pltpu.VMEM((mem_devices, 2, tile_blocks, tile), f32),
            dma((steps,)),
            dma((steps,)),
            dma,
            dma((steps, row_devices)),
            dma((steps, tiles)),
            dma((mem_devices,)),
            dma((mem_devices,)),
        ],
        compiler_params=pltpu.CompilerParams(
            collective_id=0, has_side_effects=True, vmem_limit_bytes=52 * 1024 * 1024
        ),
    )(panel, right, inverses)
    solved, remainder, spread = store(solved, remainder, spread)
    return (
        solved.T,
        jnp.swapaxes(remainder, 1, 2).reshape(right_side.shape),
        spread.reshape(tile_blocks, 1, tile),
    )


def solution(mesh):
    return jax.shard_map(
        functools.partial(shards, mesh.shape["rows"], mesh.shape["mem"]),
        mesh=mesh,
        in_specs=(P(None, "rows", None, None), P(None, "rows", None, "mem"), P()),
        out_specs=(P(None, "mem"), P(None, "rows", None, "mem"), P(None, "rows", None)),
        check_vma=False,
    )
```

```python
import functools

import jax
import jax.numpy as jnp
from jax import lax
from jax.experimental import pallas as pl
from jax.experimental.pallas import tpu as pltpu
from jax.sharding import PartitionSpec as P

f32 = jnp.float32
bf16 = jnp.bfloat16
MESH = pl.DeviceIdType.MESH


def split(x):
    high = x.astype(bf16)
    return high, (x - high.astype(f32)).astype(bf16)


def dot_nt(a, b):
    return lax.dot_general(a, b, (((1,), (1,)), ((), ())), preferred_element_type=f32)


def dot_nn(a, b):
    return lax.dot_general(a, b, (((1,), (0,)), ((), ())), preferred_element_type=f32)


def product(stacked, weight_high, weight_low, dot=dot_nt):
    half = stacked.shape[0] // 2
    both = dot(stacked, weight_high)
    return both[:half] + both[half:] + dot(stacked[:half], weight_low)


def stack(x):
    return jnp.concatenate(split(x), axis=0)


def kernel(
    row_devices,
    mem_devices,
    panel_hbm,
    right_hbm,
    inverse_hbm,
    solved,
    left,
    spread_ref,
    panel,
    inverse,
    pieces,
    gain_high,
    gain_low,
    last_high,
    last_low,
    sums,
    panel_sem,
    inverse_sem,
    right_sem,
    send_sem,
    recv_sem,
    sums_send_sem,
    sums_recv_sem,
):
    p = lax.axis_index("rows")
    m = lax.axis_index("mem")
    steps, tile_blocks, tile, width = panel.shape
    tiles = width // tile
    heads = min(tile_blocks, -(-(steps * tiles) // row_devices))
    members = left.shape[1]

    load_right = pltpu.make_async_copy(right_hbm, left, right_sem)
    load_right.start()
    load_panel, load_inverse = [], []
    for s in range(steps):
        load_inverse.append(
            pltpu.make_async_copy(inverse_hbm.at[s], inverse.at[s], inverse_sem.at[s])
        )
        load_inverse[s].start()
        load_panel.append(
            pltpu.make_async_copy(
                panel_hbm.at[:, :, pl.ds(s * width, width)], panel.at[s], panel_sem.at[s]
            )
        )
        load_panel[s].start()

    barrier = pltpu.get_barrier_semaphore()
    for k in range(1, row_devices):
        pl.semaphore_signal(
            barrier, inc=1, device_id=(lax.rem(p + k, row_devices), m), device_id_type=MESH
        )
    for k in range(1, mem_devices):
        pl.semaphore_signal(
            barrier, inc=1, device_id=(p, lax.rem(m + k, mem_devices)), device_id_type=MESH
        )
    load_right.wait()
    pl.semaphore_wait(barrier, row_devices + mem_devices - 2)

    def owner(s):
        place = p - (s * tiles) % row_devices
        return place, jnp.logical_and(place >= 0, place < tiles)

    def slot_of(s):
        return (s * tiles) // row_devices

    def copy_to(s, place, k):
        target = ((s + 1) * tiles + k) % row_devices
        return target, pltpu.make_async_remote_copy(
            src_ref=pieces.at[s, place],
            dst_ref=pieces.at[s, place],
            send_sem=send_sem.at[s, k],
            recv_sem=recv_sem.at[s, place],
            device_id=(target, m),
            device_id_type=MESH,
        )

    def send(s, residual):
        place, _ = owner(s)
        pieces[s, place] = residual
        for k in range(row_devices):
            target, copy = copy_to(s, place, k)

            @pl.when(target != p)
            def _():
                copy.start()

    def receive(s):
        for i in range(tiles):
            source = (s * tiles) % row_devices + i

            @pl.when(source != p)
            def _():
                pltpu.make_async_remote_copy(
                    src_ref=pieces.at[s, i],
                    dst_ref=pieces.at[s, i],
                    send_sem=send_sem.at[s, 0],
                    recv_sem=recv_sem.at[s, i],
                    device_id=(source, m),
                    device_id_type=MESH,
                ).wait_recv()

        return stack(jnp.concatenate([pieces[s, i] for i in range(tiles)], axis=1))

    def make_gain(s):
        load_inverse[s].wait()
        load_panel[s].wait()
        if s + 1 < steps:
            _, mine = owner(s + 1)

            @pl.when(mine)
            def _():
                high, low = split(inverse[s])
                gain = product(stack(panel[s, slot_of(s + 1)]), high, low, dot_nn)
                gain_high[s], gain_low[s] = split(gain)

    def slot_groups():
        groups = [
            (j, 1, (j * row_devices + p) // tiles >= steps) for j in range(heads)
        ]
        for j in range(heads, tile_blocks, 2):
            groups.append((j, min(2, tile_blocks - j), True))
        return groups

    def make_last():
        high, low = split(inverse[steps - 1])
        for j, count, due in slot_groups():

            @pl.when(due)
            def _():
                rows = panel[steps - 1, j : j + count].reshape(count * tile, width)
                gain = split(product(stack(rows), high, low, dot_nn))
                last_high[j * tile : (j + count) * tile] = gain[0]
                last_low[j * tile : (j + count) * tile] = gain[1]

    _, first = owner(0)

    @pl.when(first)
    def _():
        send(0, left[slot_of(0)])

    def solve(s, residual):
        high, low = split(inverse[s])
        block = product(residual, high, low)
        solved[:, s * width : (s + 1) * width] = block
        return stack(block)

    for s in range(steps):
        make_gain(s)
        if s == steps - 1:
            make_last()
        residual = receive(s)
        if s + 1 < steps:
            _, mine = owner(s + 1)

            @pl.when(mine)
            def _():
                slot = slot_of(s + 1)
                new = left[slot] - product(residual, gain_high[s], gain_low[s])
                left[slot] = new
                send(s + 1, new)

        if s == steps - 1:
            break
        block = solve(s, residual)
        for j in range(heads):
            level = (j * row_devices + p) // tiles

            @pl.when(level > s + 1)
            def _():
                high, low = split(panel[s, j])
                left[j] = left[j] - product(block, high, low)

        for j in range(heads, tile_blocks, 2):
            count = min(2, tile_blocks - j)
            high, low = split(panel[s, j : j + count].reshape(count * tile, width))
            change = product(block, high, low)
            for i in range(count):
                left[j + i] = left[j + i] - change[:, i * tile : (i + 1) * tile]

    for j, count, due in slot_groups():

        @pl.when(due)
        def _():
            rows = pl.ds(j * tile, count * tile)
            change = product(residual, last_high[rows], last_low[rows])
            for i in range(count):
                left[j + i] = left[j + i] - change[:, i * tile : (i + 1) * tile]

    value = left[...]
    sums[m] = jnp.stack([jnp.sum(value, axis=1), jnp.sum(value * value, axis=1)])

    def sums_copy(k):
        return pltpu.make_async_remote_copy(
            src_ref=sums.at[m],
            dst_ref=sums.at[m],
            send_sem=sums_send_sem.at[k],
            recv_sem=sums_recv_sem.at[m],
            device_id=(p, lax.rem(m + k, mem_devices)),
            device_id_type=MESH,
        )

    for k in range(1, mem_devices):
        sums_copy(k).start()
    solve(steps - 1, residual)
    for s in range(steps):
        place, mine = owner(s)

        @pl.when(mine)
        def _():
            for k in range(row_devices):
                target, copy = copy_to(s, place, k)

                @pl.when(target != p)
                def _():
                    copy.wait_send()

    for k in range(1, mem_devices):
        other = lax.rem(m + k, mem_devices)
        pltpu.make_async_remote_copy(
            src_ref=sums.at[other],
            dst_ref=sums.at[other],
            send_sem=sums_send_sem.at[k],
            recv_sem=sums_recv_sem.at[other],
            device_id=(p, other),
            device_id_type=MESH,
        ).wait_recv()
    total = sums[0]
    for k in range(1, mem_devices):
        total = total + sums[k]
    mean = total / (members * mem_devices)
    spread_ref[...] = mean[1] - mean[0] * mean[0]
    for k in range(1, mem_devices):
        sums_copy(k).wait_send()


def store_kernel(*refs):
    count = (len(refs) - 1) // 2
    copies = [
        pltpu.make_async_copy(refs[i], refs[count + i], refs[-1].at[i]) for i in range(count)
    ]
    for copy in copies:
        copy.start()
    for copy in copies:
        copy.wait()


def store(*arrays):
    spec = pl.BlockSpec(memory_space=pl.ANY)
    return pl.pallas_call(
        store_kernel,
        out_shape=tuple(jax.ShapeDtypeStruct(a.shape, a.dtype) for a in arrays),
        in_specs=[spec] * len(arrays),
        out_specs=(spec,) * len(arrays),
        scratch_shapes=[pltpu.SemaphoreType.DMA((len(arrays),))],
        compiler_params=pltpu.CompilerParams(vmem_limit_bytes=1024 * 1024),
    )(*arrays)


def shards(row_devices, mem_devices, factor_panel, right_side, inverses):
    tile_blocks, _, tile, columns = factor_panel.shape
    members = right_side.shape[3]
    steps, width, _ = inverses.shape
    tiles = width // tile
    panel = factor_panel.reshape(tile_blocks, tile, columns)
    right = jnp.swapaxes(right_side.reshape(tile_blocks, tile, members), 1, 2)
    hbm = pl.BlockSpec(memory_space=pltpu.HBM)
    vmem = pl.BlockSpec(memory_space=pltpu.VMEM)
    dma = pltpu.SemaphoreType.DMA
    solved, remainder, spread = pl.pallas_call(
        functools.partial(kernel, row_devices, mem_devices),
        out_shape=(
            jax.ShapeDtypeStruct((members, columns), f32),
            jax.ShapeDtypeStruct((tile_blocks, members, tile), f32),
            jax.ShapeDtypeStruct((tile_blocks, tile), f32),
        ),
        in_specs=[hbm] * 3,
        out_specs=(vmem, vmem, vmem),
        scratch_shapes=[
            pltpu.VMEM((steps, tile_blocks, tile, width), f32),
            pltpu.VMEM((steps, width, width), f32),
            pltpu.VMEM((steps, tiles, members, tile), f32),
            pltpu.VMEM((steps, tile, width), bf16),
            pltpu.VMEM((steps, tile, width), bf16),
            pltpu.VMEM((tile_blocks * tile, width), bf16),
            pltpu.VMEM((tile_blocks * tile, width), bf16),
            pltpu.VMEM((mem_devices, 2, tile_blocks, tile), f32),
            dma((steps,)),
            dma((steps,)),
            dma,
            dma((steps, row_devices)),
            dma((steps, tiles)),
            dma((mem_devices,)),
            dma((mem_devices,)),
        ],
        compiler_params=pltpu.CompilerParams(
            collective_id=0, has_side_effects=True, vmem_limit_bytes=52 * 1024 * 1024
        ),
    )(panel, right, inverses)
    solved, remainder, spread = store(solved, remainder, spread)
    return (
        solved.T,
        jnp.swapaxes(remainder, 1, 2).reshape(right_side.shape),
        spread.reshape(tile_blocks, 1, tile),
    )


def solution(mesh):
    return jax.shard_map(
        functools.partial(shards, mesh.shape["rows"], mesh.shape["mem"]),
        mesh=mesh,
        in_specs=(P(None, "rows", None, None), P(None, "rows", None, "mem"), P()),
        out_specs=(P(None, "mem"), P(None, "rows", None, "mem"), P(None, "rows", None)),
        check_vma=False,
    )
```
